256 devices in a mesh: dp: 256 (over x, y, z, core).
Axes of the slice: x: 4, y: 4, z: 8, core: 2. Of those that a mesh axis runs over, the one named last changes fastest.
Arguments:
- image_feats: bfloat16 [98304, 1152], P('dp'), may hold values from -0.26516504 to 0.26516504
- text_feats: bfloat16 [98304, 1152], P('dp'), may hold values from -0.26516504 to 0.26516504
- log_scale: float32 [], replicated, may hold values from 1.6 to 2.6
- bias: float32 [], replicated, may hold values from -5 to -2
Outputs:
- grad_image: float32 [98304, 1152], P('dp')
- grad_text: float32 [98304, 1152], P('dp')
- stats: float32 [3], replicated
The draws below stay inside these ranges and needn't reach their ends.
All inputs are finite; a program needn't handle non-finite values.
Results may differ from the reference program's by a relative error of at most 0.00058.
Values may be sent and summed in bfloat16 or wider, within the bound.
No kernel may reach another device: no remote copies, remote signals or barrier semaphores. Data moves between devices by JAX's collectives and lax.ppermute only.
A program may use at most 128 MiB of HBM per device.

```python
import jax
import jax.numpy as jnp
from jax import lax

D = 1152
ROWS_DEV = 384
STEPS = 8
TOKENS = 98304
N_DP = 256


def shared_direction(key):
    return jnp.clip(jax.random.normal(key, (D,), jnp.float32), -5.0, 5.0)


def feature_rows(key, common, top, power):
    position = jnp.arange(TOKENS, dtype=jnp.float32) / jnp.float32(TOKENS - 1)
    weight = top * position ** power
    noise = jnp.clip(jax.random.normal(key, (TOKENS, D), jnp.float32), -5.0, 5.0)
    values = (noise + weight[:, None] * common[None, :]) * D ** (-0.5)
    return values.astype(jnp.bfloat16)


def draw_image_feats(key, part):
    common = shared_direction(key)
    key = jax.random.fold_in(key, 11)
    return feature_rows(key, common, 0.8, 1.0)


def draw_text_feats(key, part):
    common = shared_direction(key)
    key = jax.random.fold_in(key, 23)
    return feature_rows(key, common, 0.8, 1.0)


def setup_inputs(seed: int = 0) -> dict:
    seeds = jax.random.split(jax.random.key(seed), 5)
    return {
        "image_feats": draw_image_feats(jax.random.fold_in(seeds[4], 71), 0),
        "text_feats": draw_text_feats(jax.random.fold_in(seeds[4], 71), 0),
        "log_scale": jnp.clip(jax.random.uniform(seeds[2], (), jnp.float32, 1.6, 2.6), 1.6, 2.6),
        "bias": jnp.clip(jax.random.uniform(seeds[3], (), jnp.float32, -5.0, -2.0), -5.0, -2.0),
    }


def normalize(raw):
    values = raw.astype(jnp.float32)
    inverse = lax.rsqrt(lax.optimization_barrier(jnp.sum(values * values, axis=-1, keepdims=True)) + 1e-06)
    return (values * inverse, inverse)

def reference(image_feats, text_feats, log_scale, bias):
    ximg, rimg = normalize(image_feats)
    xtxt, rtxt = normalize(text_feats)
    xb = ximg.astype(jnp.bfloat16).astype(jnp.float32).reshape(N_DP, ROWS_DEV, D)
    yb = xtxt.astype(jnp.bfloat16)
    scale = jnp.exp(log_scale)
    ident = jnp.eye(ROWS_DEV, dtype=jnp.float32)
    grad_x = jnp.zeros((N_DP, ROWS_DEV, D), jnp.float32)
    grad_y = jnp.zeros((TOKENS, D), jnp.float32)
    loss_sum = jnp.float32(0.0)
    scale_sum = jnp.float32(0.0)
    bias_sum = jnp.float32(0.0)
    for step in range(STEPS):
        moved = jnp.roll(yb, step * ROWS_DEV, axis=0).astype(jnp.float32).reshape(N_DP, ROWS_DEV, D)
        sim = jnp.einsum('nbd,ncd->nbc', xb, moved)
        logit = scale * sim + bias
        if step == 0:
            label = ident
        else:
            label = jnp.zeros_like(ident)
        sign = 2.0 * label - 1.0
        loss_sum = loss_sum + jnp.sum(jax.nn.softplus(-sign * logit))
        grad = jax.nn.sigmoid(logit) - label
        scale_sum = scale_sum + jnp.sum(grad * sim) * scale
        bias_sum = bias_sum + jnp.sum(grad)
        tile = (scale * grad).astype(jnp.bfloat16).astype(jnp.float32)
        grad_x = grad_x + jnp.einsum('nbc,ncd->nbd', tile, moved)
        term = jnp.einsum('nbc,nbd->ncd', tile, xb).reshape(TOKENS, D)
        grad_y = grad_y + jnp.roll(term, -step * ROWS_DEV, axis=0)
    grad_x = grad_x.reshape(TOKENS, D)
    grad_image = rimg * (grad_x - ximg * lax.optimization_barrier(jnp.sum(ximg * grad_x, axis=-1, keepdims=True)))
    grad_text = rtxt * (grad_y - xtxt * lax.optimization_barrier(jnp.sum(xtxt * grad_y, axis=-1, keepdims=True)))
    stats = jnp.stack([loss_sum, scale_sum, bias_sum]) / jnp.float32(TOKENS * STEPS)
    return (grad_image, grad_text, stats)
```

```python
import functools

import jax
import jax.numpy as jnp
from jax import lax
from jax.experimental import pallas as pl
from jax.experimental.pallas import tpu as pltpu
from jax.sharding import PartitionSpec as P

STEPS = 8
EPS = 1e-06
LOG2_E = 1.4426950408889634
LN_2 = 0.6931471805599453
ROUNDS = (1, 16, 32, 64, 128, 2, 4, 8)
VMEM_LIMIT = 24 * 1024 * 1024
SMEM = pl.BlockSpec(memory_space=pltpu.SMEM)
VMEM = pl.BlockSpec(memory_space=pltpu.VMEM)
HBM = pl.BlockSpec(memory_space=pltpu.HBM)


def my_core():
    return lax.rem(lax.axis_index("dp"), 2)


def inverse_norm(values):
    return lax.rsqrt(jnp.sum(values * values, axis=-1, keepdims=True) + EPS)


def fetch_own(x_ref, y_ref, raw, sems, want_image):
    pieces = sems.shape[0]
    size = raw.shape[0] // pieces
    for i in range(pieces):
        part = pl.ds(i * size, size)

        @pl.when(want_image)
        def _():
            pltpu.make_async_copy(x_ref.at[part], raw.at[part], sems.at[i]).start()

        @pl.when(jnp.logical_not(want_image))
        def _():
            pltpu.make_async_copy(y_ref.at[part], raw.at[part], sems.at[i]).start()


def normalize_kernel(x_ref, y_ref, a_ref, b_ref, raw, sems):
    core = my_core()
    sides = ((a_ref, core == 0), (b_ref, core == 1))
    for side, (_, want_image) in enumerate(sides):
        fetch_own(x_ref, y_ref, raw.at[side], sems.at[side], want_image)
    pieces = sems.shape[1]
    size = raw.shape[1] // pieces
    for side, (out_ref, _) in enumerate(sides):
        for i in range(pieces):
            part = pl.ds(i * size, size)
            pltpu.make_async_copy(x_ref.at[part], raw.at[side, part], sems.at[side, i]).wait()
            for start in range(i * size, (i + 1) * size, 48):
                block = slice(start, start + 48)
                values = raw[side, block, :].astype(jnp.float32)
                out_ref[block, :] = (values * inverse_norm(values)).astype(jnp.bfloat16)


def normalized(x, y):
    return pl.pallas_call(
        normalize_kernel,
        out_shape=[jax.ShapeDtypeStruct(x.shape, jnp.bfloat16)] * 2,
        in_specs=[HBM, HBM],
        out_specs=[VMEM, VMEM],
        scratch_shapes=[pltpu.VMEM((2, *x.shape), jnp.bfloat16), pltpu.SemaphoreType.DMA((2, 2))],
        compiler_params=pltpu.CompilerParams(vmem_limit_bytes=VMEM_LIMIT),
        cost_estimate=pl.CostEstimate(
            flops=4 * x.size, bytes_accessed=8 * x.size, transcendentals=0
        ),
    )(x, y)


def folded(values):
    rows, columns = values.shape
    total = jnp.sum(values.reshape(rows // 8, 8, columns), axis=0)
    out = total[:, :128]
    for start in range(128, columns, 128):
        out = out + total[:, start : start + 128]
    return out


def negatives(sim, scalars, stats, weight):
    power = jnp.exp2(sim * scalars[2] + scalars[3])
    above = 1.0 + power
    inverse = pl.reciprocal(above, approx=True)
    inverse = inverse * (2.0 - above * inverse)
    grad = power * inverse
    if stats is not None:
        rest = (power - (above - 1.0)) * inverse
        parts = (folded(jnp.log2(above)), folded(rest), folded(grad * sim), folded(grad))
        for row, part in enumerate(parts):
            stats[row * 8 : row * 8 + 8, :] += part if weight is None else part * weight
    return scalars[0] * grad


def cut(blocks, width):
    pieces, current, room = [], [], width
    for index, rows in enumerate(blocks):
        start = 0
        while start < rows:
            take = min(room, rows - start)
            current.append((index, start, take))
            start, room = start + take, room - take
            if room == 0:
                pieces.append(current)
                current, room = [], width
    if current:
        pieces.append(current)
    return pieces


def joined(blocks, piece=None):
    if piece is None:
        piece = [(i, 0, block.shape[0]) for i, block in enumerate(blocks)]
    values = [blocks[i][start : start + take, :] for i, start, take in piece]
    return values[0] if len(values) == 1 else jnp.concatenate(values, axis=0)


def stage_kernel(plan, *refs):
    modes, label, has_acc, image_core, has_outs = plan
    refs = list(refs)
    scalars, own = refs.pop(0), refs.pop(0)
    blocks = [refs.pop(0) for _ in modes]
    acc_in = refs.pop(0) if has_acc else None
    if image_core is not None:
        x_ref, y_ref = refs.pop(0), refs.pop(0)
        if has_outs:
            refs = refs[2:]
        out_image, out_text = refs.pop(0), refs.pop(0)
    else:
        acc = refs.pop(0)
    stats = refs.pop(0) if any(m is not None for m in modes) else None
    tiles = refs.pop(0)
    core = my_core()
    if image_core is not None:
        acc, raw, sems, out_sems = refs
        is_image = core == image_core
        fetch_own(x_ref, y_ref, raw, sems, is_image)
    if stats is not None:
        stats[...] = jnp.zeros_like(stats)
    weight = core.astype(jnp.float32)
    weights = {"all": None, "core1": weight, "core0": 1.0 - weight}
    rows = own.shape[0]
    column = 0
    for piece in cut([block.shape[0] for block in blocks], 256):
        other = joined(blocks, piece)
        sim = lax.dot_general(
            own[...], other, (((1,), (1,)), ((), ())), preferred_element_type=jnp.float32
        )
        offset = 0
        for i, start, take in piece:
            part = sim[:, offset : offset + take]
            mode = modes[i]
            grad = negatives(part, scalars, None if mode is None else stats, weights.get(mode))
            if label and i == 0:
                across = lax.broadcasted_iota(jnp.int32, part.shape, 0)
                along = lax.broadcasted_iota(jnp.int32, part.shape, 1) + start
                positive = across == along
                if mode is not None:
                    zero = jnp.zeros_like(part)
                    logit = scalars[0] * part + scalars[1]
                    stats[8:16, :] -= folded(jnp.where(positive, logit, zero))
                    stats[16:24, :] -= folded(jnp.where(positive, part, zero))
                    stats[24:32, :] -= folded(positive.astype(jnp.float32))
                grad = jnp.where(positive, grad - scalars[0], grad)
            tiles[:, column : column + take] = grad.astype(jnp.bfloat16)
            offset, column = offset + take, column + take
    term = jnp.dot(tiles[...], joined(blocks), preferred_element_type=jnp.float32)
    acc[...] = term if acc_in is None else acc_in[...] + term
    if image_core is None:
        return
    pieces = sems.shape[0]
    size = rows // pieces
    for i in range(pieces):
        part = pl.ds(i * size, size)
        pltpu.make_async_copy(x_ref.at[part], raw.at[part], sems.at[i]).wait()
        for start in range(i * size, (i + 1) * size, 48):
            block = slice(start, start + 48)
            values = raw[block, :].astype(jnp.float32)
            inverse = inverse_norm(values)
            unit = values * inverse
            total = acc[block, :]
            acc[block, :] = inverse * (
                total - unit * jnp.sum(unit * total, axis=-1, keepdims=True)
            )

        @pl.when(is_image)
        def _():
            pltpu.make_async_copy(acc.at[part], out_image.at[part], out_sems.at[i]).start()

        @pl.when(jnp.logical_not(is_image))
        def _():
            pltpu.make_async_copy(acc.at[part], out_text.at[part], out_sems.at[i]).start()

    for i in range(pieces):
        part = pl.ds(i * size, size)
        pltpu.make_async_copy(acc.at[part], out_image.at[part], out_sems.at[i]).wait()


def middle_kernel(plan, *refs):
    scalars, stats = refs[0], refs[-1]
    blocks = refs[1:-1]
    odd = my_core() == 1
    stats[...] = jnp.zeros_like(stats)

    def chosen(pair):
        views = [blocks[i][start : start + size, :] for i, start, size in pair]
        return views[0] if len(views) == 1 else jnp.where(odd, views[0], views[1])

    for left, right in plan:
        one, other = chosen(left), chosen(right)
        for start in range(0, other.shape[0], 256):
            sim = lax.dot_general(
                one, other[start : start + 256], (((1,), (1,)), ((), ())),
                preferred_element_type=jnp.float32,
            )
            negatives(sim, scalars, stats, None)


def middle(scalars, blocks, plan):
    rows, width = blocks[0].shape
    pairs = sum(left[0][2] * right[0][2] for left, right in plan)
    return pl.pallas_call(
        functools.partial(middle_kernel, plan),
        out_shape=jax.ShapeDtypeStruct((32, 128), jnp.float32),
        in_specs=[SMEM] + [VMEM] * len(blocks),
        out_specs=VMEM,
        compiler_params=pltpu.CompilerParams(vmem_limit_bytes=VMEM_LIMIT),
        cost_estimate=pl.CostEstimate(
            flops=2 * pairs * width, bytes_accessed=2 * rows * width, transcendentals=3 * pairs
        ),
    )(scalars, *blocks)


def stage(scalars, own, blocks, modes, acc=None, label=False, final=None):
    rows, width = own.shape
    big = jax.ShapeDtypeStruct((rows, width), jnp.float32)
    args, in_specs = [scalars, own, *blocks], [SMEM, VMEM] + [VMEM] * len(blocks)
    scratch = [pltpu.VMEM((rows, sum(block.shape[0] for block in blocks)), jnp.bfloat16)]
    aliases, image_core, has_outs = {}, None, False
    if acc is not None:
        args.append(acc)
        in_specs.append(VMEM)
    if final is None:
        if acc is not None:
            aliases = {len(args) - 1: 0}
        out_shape, out_specs = [big], [VMEM]
    else:
        image_core, x, y, outs = final
        args += [x, y]
        in_specs += [HBM, HBM]
        if outs is not None:
            has_outs = True
            aliases = {len(args): 0, len(args) + 1: 1}
            args += list(outs)
            in_specs += [HBM, HBM]
        out_shape, out_specs = [big, big], [HBM, HBM]
        scratch += [
            pltpu.VMEM((rows, width), jnp.float32),
            pltpu.VMEM((rows, width), jnp.bfloat16),
            pltpu.SemaphoreType.DMA((4,)),
            pltpu.SemaphoreType.DMA((4,)),
        ]
    if any(m is not None for m in modes):
        out_shape.append(jax.ShapeDtypeStruct((32, 128), jnp.float32))
        out_specs.append(VMEM)
    plan = (tuple(modes), label, acc is not None, image_core, has_outs)
    pairs = rows * sum(block.shape[0] for block in blocks)
    return pl.pallas_call(
        functools.partial(stage_kernel, plan),
        out_shape=out_shape,
        in_specs=in_specs,
        out_specs=out_specs,
        scratch_shapes=scratch,
        input_output_aliases=aliases,
        compiler_params=pltpu.CompilerParams(vmem_limit_bytes=VMEM_LIMIT),
        cost_estimate=pl.CostEstimate(
            flops=4 * pairs * width, bytes_accessed=10 * rows * width, transcendentals=3 * pairs
        ),
    )(*args)


def finish_kernel(divisor, scalars, stats, out_ref):
    sums = [jnp.sum(stats[row : row + 8, :]) for row in range(0, 32, 8)]
    out_ref[0] = (sums[0] * LN_2 + sums[1]) / divisor
    out_ref[1] = sums[2] * scalars[0] / divisor
    out_ref[2] = sums[3] / divisor


def finished(scalars, stats, divisor):
    return pl.pallas_call(
        functools.partial(finish_kernel, divisor),
        out_shape=jax.ShapeDtypeStruct((3,), jnp.float32),
        in_specs=[SMEM, VMEM],
        out_specs=SMEM,
    )(scalars, stats)


def tied(*values):
    return lax.optimization_barrier(values)


def per_device(image_feats, text_feats, log_scale, bias):
    count = lax.axis_size("dp")
    up_down = [(d, (d + 2 if d % 2 else d - 2) % count) for d in range(count)]
    down_up = [(d, (d - 2 if d % 2 else d + 2) % count) for d in range(count)]
    cross = [(d, (d + 1 if d % 2 else d - 1) % count) for d in range(count)]
    other_core = [(d, d ^ 1) for d in range(count)]
    scale = jnp.exp(log_scale)
    scalars = jnp.stack([scale, bias, scale * LOG2_E, bias * LOG2_E])
    x = pltpu.with_memory_space_constraint(image_feats, pltpu.HBM)
    y = pltpu.with_memory_space_constraint(text_feats, pltpu.HBM)
    rows = image_feats.shape[0]
    half = rows // 2

    def up(value):
        return lax.ppermute(value, "dp", up_down)

    def down(value):
        return lax.ppermute(value, "dp", down_up)

    def swap(value):
        return lax.ppermute(value, "dp", other_core)

    def all_added(value, rounds):
        for distance in rounds:
            if distance < count:
                pairs = [(d, d ^ distance) for d in range(count)]
                value = value + lax.ppermute(value, "dp", pairs)
        return value

    whole = lambda i: (i, 0, rows)
    a, b = normalized(x, y)
    p1 = up(a)
    r1 = down(b)
    sibling = swap(b)
    acc_a, stats0 = stage(scalars, a, [b], ["all"], label=True)

    p1, acc_a = tied(p1, acc_a)
    p2, from_p1 = up(p1), swap(p1)
    acc_b, stats1 = stage(scalars, b, [a, sibling], [None, "core1"], label=True)

    r1, from_p1, acc_b = tied(r1, from_p1, acc_b)
    r2, from_r1 = down(r1), swap(r1)
    acc_a, stats2 = stage(scalars, a, [from_p1, r1], ["core0", None], acc_a)
    stats3 = middle(scalars, [p1, r1], (((whole(0),), (whole(1),)),))

    p2, from_r1, acc_a, stats3 = tied(p2, from_r1, acc_a, stats3)
    p3, from_p2 = up(p2), swap(p2)
    acc_b, stats4 = stage(scalars, b, [p1, from_r1], ["all", "core1"], acc_b)
    stats5 = middle(
        scalars, [p1, r1, from_p1, from_r1, p2],
        (
            ((whole(0), whole(1)), (whole(2), whole(3))),
            ((whole(4),), (whole(1),)),
        ),
    )

    r2, from_p2, acc_b, stats5 = tied(r2, from_p2, acc_b, stats5)
    r3, from_r2 = down(r2), swap(r2)
    stats6 = middle(
        scalars, [p2, r2, from_p1, from_r1, from_p2],
        (
            ((whole(0), whole(1)), (whole(2), whole(3))),
            (((0, 0, half), (4, half, half)), (whole(4), whole(0))),
        ),
    )
    stats = stats0 + stats1 + stats2 + stats3 + stats4 + stats5 + stats6
    stats = all_added(stats, ROUNDS[:1])
    (acc_a,) = stage(scalars, a, [from_p2, r2], [None, None], acc_a)

    p3, from_r2, acc_a, stats = tied(p3, from_r2, acc_a, stats)
    last, from_p3 = lax.ppermute(p3, "dp", cross), swap(p3)
    stats = all_added(stats, ROUNDS[1:3])
    (acc_b,) = stage(scalars, b, [p2, from_r2], [None, None], acc_b)

    r3, from_p3, acc_b, stats = tied(r3, from_p3, acc_b, stats)
    from_r3 = [swap(r3[:half]), swap(r3[half:])]
    stats = all_added(stats, ROUNDS[3:5])
    (acc_a,) = stage(scalars, a, [from_p3, r3], [None, None], acc_a)

    from_r3, acc_a, stats = tied(from_r3, acc_a, stats)
    outs = stage(
        scalars, b, [p3, *from_r3], [None, None, None], acc_b,
        final=(1, x, y, None),
    )
    stats = all_added(stats, ROUNDS[5:])
    sums = finished(scalars, stats, float(rows * count * STEPS))
    last, sums = tied(last, sums)
    grad_image, grad_text = stage(
        scalars, a, [last], [None], acc_a, final=(0, x, y, outs)
    )
    return grad_image, grad_text, sums


def solution(mesh):
    in_specs = (P("dp", None), P("dp", None), P(), P())
    out_specs = (P("dp", None), P("dp", None), P())
    return jax.shard_map(
        per_device, mesh=mesh, in_specs=in_specs, out_specs=out_specs, check_vma=False
    )
```

```python
import functools

import jax
import jax.numpy as jnp
from jax import lax
from jax.experimental import pallas as pl
from jax.experimental.pallas import tpu as pltpu
from jax.sharding import PartitionSpec as P

STEPS = 8
EPS = 1e-06
LOG2_E = 1.4426950408889634
LN_2 = 0.6931471805599453
ROUNDS = ((16,), (32,), (64,), (128,), (2,), (4,), (8,), 1)
VMEM_LIMIT = 24 * 1024 * 1024
SMEM = pl.BlockSpec(memory_space=pltpu.SMEM)
VMEM = pl.BlockSpec(memory_space=pltpu.VMEM)
HBM = pl.BlockSpec(memory_space=pltpu.HBM)


def my_core():
    return lax.rem(lax.axis_index("dp"), 2)


def inverse_norm(values):
    return lax.rsqrt(jnp.sum(values * values, axis=-1, keepdims=True) + EPS)


def fetch_own(x_ref, y_ref, raw, sems, want_image):
    pieces = sems.shape[0]
    size = raw.shape[0] // pieces
    for i in range(pieces):
        part = pl.ds(i * size, size)

        @pl.when(want_image)
        def _():
            pltpu.make_async_copy(x_ref.at[part], raw.at[part], sems.at[i]).start()

        @pl.when(jnp.logical_not(want_image))
        def _():
            pltpu.make_async_copy(y_ref.at[part], raw.at[part], sems.at[i]).start()


def normalize_kernel(x_ref, y_ref, a_ref, b_ref, raw, sems):
    core = my_core()
    sides = ((a_ref, core == 0), (b_ref, core == 1))
    for side, (_, want_image) in enumerate(sides):
        fetch_own(x_ref, y_ref, raw.at[side], sems.at[side], want_image)
    pieces = sems.shape[1]
    size = raw.shape[1] // pieces
    for side, (out_ref, _) in enumerate(sides):
        for i in range(pieces):
            part = pl.ds(i * size, size)
            pltpu.make_async_copy(x_ref.at[part], raw.at[side, part], sems.at[side, i]).wait()
            for start in range(i * size, (i + 1) * size, 48):
                block = slice(start, start + 48)
                values = raw[side, block, :].astype(jnp.float32)
                out_ref[block, :] = (values * inverse_norm(values)).astype(jnp.bfloat16)


def normalized(x, y):
    return pl.pallas_call(
        normalize_kernel,
        out_shape=[jax.ShapeDtypeStruct(x.shape, jnp.bfloat16)] * 2,
        in_specs=[HBM, HBM],
        out_specs=[VMEM, VMEM],
        scratch_shapes=[pltpu.VMEM((2, *x.shape), jnp.bfloat16), pltpu.SemaphoreType.DMA((2, 2))],
        compiler_params=pltpu.CompilerParams(vmem_limit_bytes=VMEM_LIMIT),
        cost_estimate=pl.CostEstimate(flops=1, bytes_accessed=1, transcendentals=0),
    )(x, y)


def folded(values):
    rows, columns = values.shape
    total = jnp.sum(values.reshape(rows // 8, 8, columns), axis=0)
    out = total[:, :128]
    for start in range(128, columns, 128):
        out = out + total[:, start : start + 128]
    return out


def negatives(sim, scalars, stats, weight):
    power = jnp.exp2(sim * scalars[2] + scalars[3])
    above = 1.0 + power
    inverse = pl.reciprocal(above, approx=True)
    inverse = inverse * (2.0 - above * inverse)
    grad = power * inverse
    if stats is not None:
        rest = (power - (above - 1.0)) * inverse
        parts = (folded(jnp.log2(above)), folded(rest), folded(grad * sim), folded(grad))
        for row, part in enumerate(parts):
            stats[row * 8 : row * 8 + 8, :] += part if weight is None else part * weight
    return scalars[0] * grad


def cut(blocks, width):
    pieces, current, room = [], [], width
    for index, rows in enumerate(blocks):
        start = 0
        while start < rows:
            take = min(room, rows - start)
            current.append((index, start, take))
            start, room = start + take, room - take
            if room == 0:
                pieces.append(current)
                current, room = [], width
    if current:
        pieces.append(current)
    return pieces


def joined(blocks, piece=None):
    if piece is None:
        piece = [(i, 0, block.shape[0]) for i, block in enumerate(blocks)]
    values = [blocks[i][start : start + take, :] for i, start, take in piece]
    return values[0] if len(values) == 1 else jnp.concatenate(values, axis=0)


def stage_kernel(plan, *refs):
    modes, label, has_acc, image_core, has_outs = plan
    refs = list(refs)
    scalars, own = refs.pop(0), refs.pop(0)
    blocks = [refs.pop(0) for _ in modes]
    acc_in = refs.pop(0) if has_acc else None
    if image_core is not None:
        x_ref, y_ref = refs.pop(0), refs.pop(0)
        if has_outs:
            refs = refs[2:]
        out_image, out_text = refs.pop(0), refs.pop(0)
    else:
        acc = refs.pop(0)
    stats = refs.pop(0) if any(m is not None for m in modes) else None
    tiles = refs.pop(0)
    core = my_core()
    if image_core is not None:
        acc, raw, sems, out_sems = refs
        is_image = core == image_core
        fetch_own(x_ref, y_ref, raw, sems, is_image)
    if stats is not None:
        stats[...] = jnp.zeros_like(stats)
    weight = core.astype(jnp.float32)
    weights = {"all": None, "core1": weight, "core0": 1.0 - weight}
    rows = own.shape[0]
    column = 0
    for piece in cut([block.shape[0] for block in blocks], 256):
        other = joined(blocks, piece)
        sim = lax.dot_general(
            own[...], other, (((1,), (1,)), ((), ())), preferred_element_type=jnp.float32
        )
        offset = 0
        for i, start, take in piece:
            part = sim[:, offset : offset + take]
            mode = modes[i]
            grad = negatives(part, scalars, None if mode is None else stats, weights.get(mode))
            if label and i == 0:
                across = lax.broadcasted_iota(jnp.int32, part.shape, 0)
                along = lax.broadcasted_iota(jnp.int32, part.shape, 1) + start
                positive = across == along
                if mode is not None:
                    zero = jnp.zeros_like(part)
                    logit = scalars[0] * part + scalars[1]
                    stats[8:16, :] -= folded(jnp.where(positive, logit, zero))
                    stats[16:24, :] -= folded(jnp.where(positive, part, zero))
                    stats[24:32, :] -= folded(positive.astype(jnp.float32))
                grad = jnp.where(positive, grad - scalars[0], grad)
            tiles[:, column : column + take] = grad.astype(jnp.bfloat16)
            offset, column = offset + take, column + take
    term = jnp.dot(tiles[...], joined(blocks), preferred_element_type=jnp.float32)
    acc[...] = term if acc_in is None else acc_in[...] + term
    if image_core is None:
        return
    pieces = sems.shape[0]
    size = rows // pieces
    for i in range(pieces):
        part = pl.ds(i * size, size)
        pltpu.make_async_copy(x_ref.at[part], raw.at[part], sems.at[i]).wait()
        for start in range(i * size, (i + 1) * size, 48):
            block = slice(start, start + 48)
            values = raw[block, :].astype(jnp.float32)
            inverse = inverse_norm(values)
            unit = values * inverse
            total = acc[block, :]
            acc[block, :] = inverse * (
                total - unit * jnp.sum(unit * total, axis=-1, keepdims=True)
            )

        @pl.when(is_image)
        def _():
            pltpu.make_async_copy(acc.at[part], out_image.at[part], out_sems.at[i]).start()

        @pl.when(jnp.logical_not(is_image))
        def _():
            pltpu.make_async_copy(acc.at[part], out_text.at[part], out_sems.at[i]).start()

    for i in range(pieces):
        part = pl.ds(i * size, size)
        pltpu.make_async_copy(acc.at[part], out_image.at[part], out_sems.at[i]).wait()


def middle_kernel(plan, *refs):
    scalars, stats = refs[0], refs[-1]
    blocks = refs[1:-1]
    odd = my_core() == 1
    stats[...] = jnp.zeros_like(stats)

    def chosen(pair):
        views = [blocks[i][start : start + size, :] for i, start, size in pair]
        return views[0] if len(views) == 1 else jnp.where(odd, views[0], views[1])

    for left, right in plan:
        one, other = chosen(left), chosen(right)
        for start in range(0, other.shape[0], 256):
            sim = lax.dot_general(
                one, other[start : start + 256], (((1,), (1,)), ((), ())),
                preferred_element_type=jnp.float32,
            )
            negatives(sim, scalars, stats, None)


def middle(scalars, blocks, plan):
    rows, width = blocks[0].shape
    pairs = sum(left[0][2] * right[0][2] for left, right in plan)
    return pl.pallas_call(
        functools.partial(middle_kernel, plan),
        out_shape=jax.ShapeDtypeStruct((32, 128), jnp.float32),
        in_specs=[SMEM] + [VMEM] * len(blocks),
        out_specs=VMEM,
        compiler_params=pltpu.CompilerParams(vmem_limit_bytes=VMEM_LIMIT),
        cost_estimate=pl.CostEstimate(flops=1, bytes_accessed=1, transcendentals=0),
    )(scalars, *blocks)


def stage(scalars, own, blocks, modes, acc=None, label=False, final=None):
    rows, width = own.shape
    big = jax.ShapeDtypeStruct((rows, width), jnp.float32)
    args, in_specs = [scalars, own, *blocks], [SMEM, VMEM] + [VMEM] * len(blocks)
    scratch = [pltpu.VMEM((rows, sum(block.shape[0] for block in blocks)), jnp.bfloat16)]
    aliases, image_core, has_outs = {}, None, False
    if acc is not None:
        args.append(acc)
        in_specs.append(VMEM)
    if final is None:
        if acc is not None:
            aliases = {len(args) - 1: 0}
        out_shape, out_specs = [big], [VMEM]
    else:
        image_core, x, y, outs = final
        args += [x, y]
        in_specs += [HBM, HBM]
        if outs is not None:
            has_outs = True
            aliases = {len(args): 0, len(args) + 1: 1}
            args += list(outs)
            in_specs += [HBM, HBM]
        out_shape, out_specs = [big, big], [HBM, HBM]
        scratch += [
            pltpu.VMEM((rows, width), jnp.float32),
            pltpu.VMEM((rows, width), jnp.bfloat16),
            pltpu.SemaphoreType.DMA((4,)),
            pltpu.SemaphoreType.DMA((4,)),
        ]
    if any(m is not None for m in modes):
        out_shape.append(jax.ShapeDtypeStruct((32, 128), jnp.float32))
        out_specs.append(VMEM)
    plan = (tuple(modes), label, acc is not None, image_core, has_outs)
    pairs = rows * sum(block.shape[0] for block in blocks)
    return pl.pallas_call(
        functools.partial(stage_kernel, plan),
        out_shape=out_shape,
        in_specs=in_specs,
        out_specs=out_specs,
        scratch_shapes=scratch,
        input_output_aliases=aliases,
        compiler_params=pltpu.CompilerParams(vmem_limit_bytes=VMEM_LIMIT),
        cost_estimate=pl.CostEstimate(flops=1, bytes_accessed=1, transcendentals=0),
    )(*args)


def finish_kernel(divisor, scalars, mine, theirs, out_ref):
    total = mine[...] + theirs[...]
    sums = [jnp.sum(total[row : row + 8, :]) for row in range(0, 32, 8)]
    out_ref[0] = (sums[0] * LN_2 + sums[1]) / divisor
    out_ref[1] = sums[2] * scalars[0] / divisor
    out_ref[2] = sums[3] / divisor


def finished(scalars, mine, theirs, divisor):
    return pl.pallas_call(
        functools.partial(finish_kernel, divisor),
        out_shape=jax.ShapeDtypeStruct((3,), jnp.float32),
        in_specs=[SMEM, VMEM, VMEM],
        out_specs=SMEM,
    )(scalars, mine, theirs)


def tied(*values):
    return lax.optimization_barrier(values)


def per_device(image_feats, text_feats, log_scale, bias):
    count = lax.axis_size("dp")
    up_down = [(d, (d + 2 if d % 2 else d - 2) % count) for d in range(count)]
    down_up = [(d, (d - 2 if d % 2 else d + 2) % count) for d in range(count)]
    cross = [(d, (d + 1 if d % 2 else d - 1) % count) for d in range(count)]
    other_core = [(d, d ^ 1) for d in range(count)]
    scale = jnp.exp(log_scale)
    scalars = jnp.stack([scale, bias, scale * LOG2_E, bias * LOG2_E])
    x = pltpu.with_memory_space_constraint(image_feats, pltpu.HBM)
    y = pltpu.with_memory_space_constraint(text_feats, pltpu.HBM)
    rows = image_feats.shape[0]
    half = rows // 2

    def up(value):
        return lax.ppermute(value, "dp", up_down)

    def down(value):
        return lax.ppermute(value, "dp", down_up)

    def swap(value):
        return lax.ppermute(value, "dp", other_core)

    def exchanged(value, distance):
        return lax.ppermute(value, "dp", [(d, d ^ distance) for d in range(count)])

    def all_added(value, distances):
        for distance in distances:
            if distance < count:
                value = value + exchanged(value, distance)
        return value

    whole = lambda i: (i, 0, rows)
    a, b = normalized(x, y)
    p1 = up(a)
    sibling = swap(b)
    acc_a, stats0 = stage(scalars, a, [b], ["all"], label=True)
    b, acc_a = tied(b, acc_a)
    r1 = down(b)
    acc_b, stats1 = stage(scalars, b, [a, sibling], [None, "core1"], label=True)

    p1, acc_a, acc_b = tied(p1, acc_a, acc_b)
    p2, from_p1 = up(p1), swap(p1)
    acc_b, stats2 = stage(scalars, b, [p1], ["all"], acc_b)

    r1, acc_b = tied(r1, acc_b)
    r2, from_r1 = down(r1), swap(r1)
    (acc_a,) = stage(scalars, a, [r1], [None], acc_a)
    stats3 = middle(scalars, [p1, r1], (((whole(0),), (whole(1),)),))

    p2, from_p1, acc_a, stats3 = tied(p2, from_p1, acc_a, stats3)
    p3, from_p2 = up(p2), swap(p2)
    acc_a, stats4 = stage(scalars, a, [from_p1], ["core0"], acc_a)
    stats5 = middle(scalars, [p2, r1], (((whole(0),), (whole(1),)),))

    r2, from_r1, acc_a, stats5 = tied(r2, from_r1, acc_a, stats5)
    r3, from_r2 = down(r2), swap(r2)
    acc_b, stats6 = stage(scalars, b, [from_r1], ["core1"], acc_b)
    stats7 = middle(
        scalars, [p1, r1, p2, r2, from_p1, from_r1, from_p2],
        (
            ((whole(0), whole(1)), (whole(4), whole(5))),
            ((whole(2), whole(3)), (whole(4), whole(5))),
            (((2, 0, half), (6, half, half)), (whole(6), whole(2))),
        ),
    )
    stats = (stats0 + stats1 + stats2 + stats3) + (stats4 + stats5 + stats6 + stats7)
    rounds = iter(ROUNDS)
    stats, acc_a, acc_b = tied(stats, acc_a, acc_b)
    stats = all_added(stats, next(rounds))
    (acc_a,) = stage(scalars, a, [r2], [None], acc_a)
    stats, acc_a, acc_b = tied(stats, acc_a, acc_b)
    stats = all_added(stats, next(rounds))
    (acc_a,) = stage(scalars, a, [from_p2], [None], acc_a)

    p3, acc_a, acc_b, stats = tied(p3, acc_a, acc_b, stats)
    last, from_p3 = lax.ppermute(p3, "dp", cross), swap(p3)
    stats = all_added(stats, next(rounds))
    (acc_b,) = stage(scalars, b, [p2], [None], acc_b)
    stats, acc_a, acc_b = tied(stats, acc_a, acc_b)
    stats = all_added(stats, next(rounds))
    (acc_b,) = stage(scalars, b, [from_r2], [None], acc_b)

    r3, acc_a, acc_b, stats = tied(r3, acc_a, acc_b, stats)
    from_r3 = [swap(r3[:half]), swap(r3[half:])]
    stats = all_added(stats, next(rounds))
    (acc_a,) = stage(scalars, a, [r3], [None], acc_a)
    stats, acc_a, acc_b = tied(stats, acc_a, acc_b)
    stats = all_added(stats, next(rounds))
    (acc_a,) = stage(scalars, a, [from_p3], [None], acc_a)
    stats, acc_a, acc_b = tied(stats, acc_a, acc_b)
    stats = all_added(stats, next(rounds))
    outs = stage(
        scalars, b, [p3, *from_r3], [None, None, None], acc_b, final=(1, x, y, None)
    )

    last, outs, stats = tied(last, outs, stats)
    theirs = exchanged(stats, next(rounds))
    grad_image, grad_text = stage(
        scalars, a, [last], [None], acc_a, final=(0, x, y, tuple(outs))
    )
    sums = finished(scalars, stats, theirs, float(rows * count * STEPS))
    return grad_image, grad_text, sums


def solution(mesh):
    in_specs = (P("dp", None), P("dp", None), P(), P())
    out_specs = (P("dp", None), P("dp", None), P())
    return jax.shard_map(
        per_device, mesh=mesh, in_specs=in_specs, out_specs=out_specs, check_vma=False
    )
```

```python
import functools

import jax
import jax.numpy as jnp
from jax import lax
from jax.experimental import pallas as pl
from jax.experimental.pallas import tpu as pltpu
from jax.sharding import PartitionSpec as P

STEPS = 8
EPS = 1e-06
LOG2_E = 1.4426950408889634
LN_2 = 0.6931471805599453
ROUNDS = ((16,), (32,), (64,), (128,), (2,), (4,), (8,), 1)
VMEM_LIMIT = 24 * 1024 * 1024
SMEM = pl.BlockSpec(memory_space=pltpu.SMEM)
VMEM = pl.BlockSpec(memory_space=pltpu.VMEM)
HBM = pl.BlockSpec(memory_space=pltpu.HBM)


def my_core():
    return lax.rem(lax.axis_index("dp"), 2)


def inverse_norm(values):
    return lax.rsqrt(jnp.sum(values * values, axis=-1, keepdims=True) + EPS)


def fetch_own(x_ref, y_ref, raw, sems, want_image):
    pieces = sems.shape[0]
    size = raw.shape[0] // pieces
    for i in range(pieces):
        part = pl.ds(i * size, size)

        @pl.when(want_image)
        def _():
            pltpu.make_async_copy(x_ref.at[part], raw.at[part], sems.at[i]).start()

        @pl.when(jnp.logical_not(want_image))
        def _():
            pltpu.make_async_copy(y_ref.at[part], raw.at[part], sems.at[i]).start()


def normalize_kernel(x_ref, y_ref, a_ref, b_ref, raw, sems):
    core = my_core()
    sides = ((a_ref, core == 0), (b_ref, core == 1))
    for side, (_, want_image) in enumerate(sides):
        fetch_own(x_ref, y_ref, raw.at[side], sems.at[side], want_image)
    pieces = sems.shape[1]
    size = raw.shape[1] // pieces
    for side, (out_ref, _) in enumerate(sides):
        for i in range(pieces):
            part = pl.ds(i * size, size)
            pltpu.make_async_copy(x_ref.at[part], raw.at[side, part], sems.at[side, i]).wait()
            for start in range(i * size, (i + 1) * size, 48):
                block = slice(start, start + 48)
                values = raw[side, block, :].astype(jnp.float32)
                out_ref[block, :] = (values * inverse_norm(values)).astype(jnp.bfloat16)


def normalized(x, y):
    return pl.pallas_call(
        normalize_kernel,
        out_shape=[jax.ShapeDtypeStruct(x.shape, jnp.bfloat16)] * 2,
        in_specs=[HBM, HBM],
        out_specs=[VMEM, VMEM],
        scratch_shapes=[pltpu.VMEM((2, *x.shape), jnp.bfloat16), pltpu.SemaphoreType.DMA((2, 2))],
        compiler_params=pltpu.CompilerParams(vmem_limit_bytes=VMEM_LIMIT),
        cost_estimate=pl.CostEstimate(flops=1, bytes_accessed=1, transcendentals=0),
    )(x, y)


def folded(values):
    rows, columns = values.shape
    total = jnp.sum(values.reshape(rows // 8, 8, columns), axis=0)
    out = total[:, :128]
    for start in range(128, columns, 128):
        out = out + total[:, start : start + 128]
    return out


def negatives(sim, scalars, stats, weight):
    power = jnp.exp2(sim * scalars[2] + scalars[3])
    above = 1.0 + power
    inverse = pl.reciprocal(above, approx=True)
    inverse = inverse * (2.0 - above * inverse)
    grad = power * inverse
    if stats is not None:
        rest = (power - (above - 1.0)) * inverse
        parts = (folded(jnp.log2(above)), folded(rest), folded(grad * sim), folded(grad))
        for row, part in enumerate(parts):
            stats[row * 8 : row * 8 + 8, :] += part if weight is None else part * weight
    return scalars[0] * grad


def cut(blocks, width):
    pieces, current, room = [], [], width
    for index, rows in enumerate(blocks):
        start = 0
        while start < rows:
            take = min(room, rows - start)
            current.append((index, start, take))
            start, room = start + take, room - take
            if room == 0:
                pieces.append(current)
                current, room = [], width
    if current:
        pieces.append(current)
    return pieces


def joined(blocks, piece=None):
    if piece is None:
        piece = [(i, 0, block.shape[0]) for i, block in enumerate(blocks)]
    values = [blocks[i][start : start + take, :] for i, start, take in piece]
    return values[0] if len(values) == 1 else jnp.concatenate(values, axis=0)


def stage_kernel(plan, *refs):
    modes, label, has_acc, image_core, has_outs = plan
    refs = list(refs)
    scalars, own = refs.pop(0), refs.pop(0)
    blocks = [refs.pop(0) for _ in modes]
    acc_in = refs.pop(0) if has_acc else None
    if image_core is not None:
        x_ref, y_ref = refs.pop(0), refs.pop(0)
        if has_outs:
            refs = refs[2:]
        out_image, out_text = refs.pop(0), refs.pop(0)
    else:
        acc = refs.pop(0)
    stats = refs.pop(0) if any(m is not None for m in modes) else None
    tiles = refs.pop(0)
    core = my_core()
    if image_core is not None:
        acc, raw, sems, out_sems = refs
        is_image = core == image_core
        fetch_own(x_ref, y_ref, raw, sems, is_image)
    if stats is not None:
        stats[...] = jnp.zeros_like(stats)
    weight = core.astype(jnp.float32)
    weights = {"all": None, "core1": weight, "core0": 1.0 - weight}
    rows = own.shape[0]
    column = 0
    for piece in cut([block.shape[0] for block in blocks], 256):
        other = joined(blocks, piece)
        sim = lax.dot_general(
            own[...], other, (((1,), (1,)), ((), ())), preferred_element_type=jnp.float32
        )
        offset = 0
        for i, start, take in piece:
            part = sim[:, offset : offset + take]
            mode = modes[i]
            grad = negatives(part, scalars, None if mode is None else stats, weights.get(mode))
            if label and i == 0:
                across = lax.broadcasted_iota(jnp.int32, part.shape, 0)
                along = lax.broadcasted_iota(jnp.int32, part.shape, 1) + start
                positive = across == along
                if mode is not None:
                    zero = jnp.zeros_like(part)
                    logit = scalars[0] * part + scalars[1]
                    stats[8:16, :] -= folded(jnp.where(positive, logit, zero))
                    stats[16:24, :] -= folded(jnp.where(positive, part, zero))
                    stats[24:32, :] -= folded(positive.astype(jnp.float32))
                grad = jnp.where(positive, grad - scalars[0], grad)
            tiles[:, column : column + take] = grad.astype(jnp.bfloat16)
            offset, column = offset + take, column + take
    term = jnp.dot(tiles[...], joined(blocks), preferred_element_type=jnp.float32)
    acc[...] = term if acc_in is None else acc_in[...] + term
    if image_core is None:
        return
    pieces = sems.shape[0]
    size = rows // pieces
    for i in range(pieces):
        part = pl.ds(i * size, size)
        pltpu.make_async_copy(x_ref.at[part], raw.at[part], sems.at[i]).wait()
        for start in range(i * size, (i + 1) * size, 48):
            block = slice(start, start + 48)
            values = raw[block, :].astype(jnp.float32)
            inverse = inverse_norm(values)
            unit = values * inverse
            total = acc[block, :]
            acc[block, :] = inverse * (
                total - unit * jnp.sum(unit * total, axis=-1, keepdims=True)
            )

        @pl.when(is_image)
        def _():
            pltpu.make_async_copy(acc.at[part], out_image.at[part], out_sems.at[i]).start()

        @pl.when(jnp.logical_not(is_image))
        def _():
            pltpu.make_async_copy(acc.at[part], out_text.at[part], out_sems.at[i]).start()

    for i in range(pieces):
        part = pl.ds(i * size, size)
        pltpu.make_async_copy(acc.at[part], out_image.at[part], out_sems.at[i]).wait()


def middle_kernel(plan, *refs):
    scalars, stats = refs[0], refs[-1]
    blocks = refs[1:-1]
    odd = my_core() == 1
    stats[...] = jnp.zeros_like(stats)

    def chosen(pair):
        views = [blocks[i][start : start + size, :] for i, start, size in pair]
        return views[0] if len(views) == 1 else jnp.where(odd, views[0], views[1])

    for left, right in plan:
        one, other = chosen(left), chosen(right)
        for start in range(0, other.shape[0], 256):
            sim = lax.dot_general(
                one, other[start : start + 256], (((1,), (1,)), ((), ())),
                preferred_element_type=jnp.float32,
            )
            negatives(sim, scalars, stats, None)


def middle(scalars, blocks, plan):
    rows, width = blocks[0].shape
    pairs = sum(left[0][2] * right[0][2] for left, right in plan)
    return pl.pallas_call(
        functools.partial(middle_kernel, plan),
        out_shape=jax.ShapeDtypeStruct((32, 128), jnp.float32),
        in_specs=[SMEM] + [VMEM] * len(blocks),
        out_specs=VMEM,
        compiler_params=pltpu.CompilerParams(vmem_limit_bytes=VMEM_LIMIT),
        cost_estimate=pl.CostEstimate(flops=1, bytes_accessed=1, transcendentals=0),
    )(scalars, *blocks)


def stage(scalars, own, blocks, modes, acc=None, label=False, final=None):
    rows, width = own.shape
    big = jax.ShapeDtypeStruct((rows, width), jnp.float32)
    args, in_specs = [scalars, own, *blocks], [SMEM, VMEM] + [VMEM] * len(blocks)
    scratch = [pltpu.VMEM((rows, sum(block.shape[0] for block in blocks)), jnp.bfloat16)]
    aliases, image_core, has_outs = {}, None, False
    if acc is not None:
        args.append(acc)
        in_specs.append(VMEM)
    if final is None:
        if acc is not None:
            aliases = {len(args) - 1: 0}
        out_shape, out_specs = [big], [VMEM]
    else:
        image_core, x, y, outs = final
        args += [x, y]
        in_specs += [HBM, HBM]
        if outs is not None:
            has_outs = True
            aliases = {len(args): 0, len(args) + 1: 1}
            args += list(outs)
            in_specs += [HBM, HBM]
        out_shape, out_specs = [big, big], [HBM, HBM]
        scratch += [
            pltpu.VMEM((rows, width), jnp.float32),
            pltpu.VMEM((rows, width), jnp.bfloat16),
            pltpu.SemaphoreType.DMA((4,)),
            pltpu.SemaphoreType.DMA((4,)),
        ]
    if any(m is not None for m in modes):
        out_shape.append(jax.ShapeDtypeStruct((32, 128), jnp.float32))
        out_specs.append(VMEM)
    plan = (tuple(modes), label, acc is not None, image_core, has_outs)
    pairs = rows * sum(block.shape[0] for block in blocks)
    return pl.pallas_call(
        functools.partial(stage_kernel, plan),
        out_shape=out_shape,
        in_specs=in_specs,
        out_specs=out_specs,
        scratch_shapes=scratch,
        input_output_aliases=aliases,
        compiler_params=pltpu.CompilerParams(vmem_limit_bytes=VMEM_LIMIT),
        cost_estimate=pl.CostEstimate(flops=1, bytes_accessed=1, transcendentals=0),
    )(*args)


def finish_kernel(divisor, scalars, mine, theirs, out_ref):
    total = mine[...] + theirs[...]
    sums = [jnp.sum(total[row : row + 8, :]) for row in range(0, 32, 8)]
    out_ref[0] = (sums[0] * LN_2 + sums[1]) / divisor
    out_ref[1] = sums[2] * scalars[0] / divisor
    out_ref[2] = sums[3] / divisor


def finished(scalars, mine, theirs, divisor):
    return pl.pallas_call(
        functools.partial(finish_kernel, divisor),
        out_shape=jax.ShapeDtypeStruct((3,), jnp.float32),
        in_specs=[SMEM, VMEM, VMEM],
        out_specs=SMEM,
    )(scalars, mine, theirs)


def tied(*values):
    return lax.optimization_barrier(values)


def per_device(image_feats, text_feats, log_scale, bias):
    count = lax.axis_size("dp")
    up_down = [(d, (d + 2 if d % 2 else d - 2) % count) for d in range(count)]
    down_up = [(d, (d - 2 if d % 2 else d + 2) % count) for d in range(count)]
    cross = [(d, (d + 1 if d % 2 else d - 1) % count) for d in range(count)]
    other_core = [(d, d ^ 1) for d in range(count)]
    scale = jnp.exp(log_scale)
    scalars = jnp.stack([scale, bias, scale * LOG2_E, bias * LOG2_E])
    x = pltpu.with_memory_space_constraint(image_feats, pltpu.HBM)
    y = pltpu.with_memory_space_constraint(text_feats, pltpu.HBM)
    rows = image_feats.shape[0]
    half = rows // 2

    def up(value):
        return lax.ppermute(value, "dp", up_down)

    def down(value):
        return lax.ppermute(value, "dp", down_up)

    def swap(value):
        return lax.ppermute(value, "dp", other_core)

    def exchanged(value, distance):
        return lax.ppermute(value, "dp", [(d, d ^ distance) for d in range(count)])

    def all_added(value, distances):
        for distance in distances:
            if distance < count:
                value = value + exchanged(value, distance)
        return value

    whole = lambda i: (i, 0, rows)
    a, b = normalized(x, y)
    p1 = up(a)
    sibling = swap(b)
    acc_a, stats0 = stage(scalars, a, [b], ["all"], label=True)
    acc_b, stats1 = stage(scalars, b, [a, sibling], [None, "core1"], label=True)
    b, acc_a, acc_b = tied(b, acc_a, acc_b)
    r1 = down(b)

    p1, acc_a, acc_b = tied(p1, acc_a, acc_b)
    p2, from_p1 = up(p1), swap(p1)
    acc_b, stats2 = stage(scalars, b, [p1], ["all"], acc_b)

    r1, acc_b = tied(r1, acc_b)
    r2, from_r1 = down(r1), swap(r1)
    (acc_a,) = stage(scalars, a, [r1], [None], acc_a)
    stats3 = middle(scalars, [p1, r1], (((whole(0),), (whole(1),)),))

    p2, from_p1, acc_a, stats3 = tied(p2, from_p1, acc_a, stats3)
    p3, from_p2 = up(p2), swap(p2)
    acc_a, stats4 = stage(scalars, a, [from_p1], ["core0"], acc_a)
    stats5 = middle(scalars, [p2, r1], (((whole(0),), (whole(1),)),))

    r2, from_r1, acc_a, stats5 = tied(r2, from_r1, acc_a, stats5)
    r3, from_r2 = down(r2), swap(r2)
    acc_b, stats6 = stage(scalars, b, [from_r1], ["core1"], acc_b)
    stats7 = middle(
        scalars, [p1, r1, p2, r2, from_p1, from_r1, from_p2],
        (
            ((whole(0), whole(1)), (whole(4), whole(5))),
            ((whole(2), whole(3)), (whole(4), whole(5))),
            (((2, 0, half), (6, half, half)), (whole(6), whole(2))),
        ),
    )
    stats = (stats0 + stats1 + stats2 + stats3) + (stats4 + stats5 + stats6 + stats7)
    rounds = iter(ROUNDS)
    stats, acc_a, acc_b = tied(stats, acc_a, acc_b)
    stats = all_added(stats, next(rounds))
    (acc_a,) = stage(scalars, a, [r2], [None], acc_a)
    stats, acc_a, acc_b = tied(stats, acc_a, acc_b)
    stats = all_added(stats, next(rounds))
    (acc_a,) = stage(scalars, a, [from_p2], [None], acc_a)

    p3, acc_a, acc_b, stats = tied(p3, acc_a, acc_b, stats)
    last, from_p3 = lax.ppermute(p3, "dp", cross), swap(p3)
    stats = all_added(stats, next(rounds))
    (acc_b,) = stage(scalars, b, [p2], [None], acc_b)
    from_r2, stats, acc_a, acc_b = tied(from_r2, stats, acc_a, acc_b)
    stats = all_added(stats, next(rounds))
    (acc_b,) = stage(scalars, b, [from_r2], [None], acc_b)

    r3, acc_a, acc_b, stats = tied(r3, acc_a, acc_b, stats)
    from_r3 = [swap(r3[:half]), swap(r3[half:])]
    stats = all_added(stats, next(rounds))
    (acc_a,) = stage(scalars, a, [r3], [None], acc_a)
    from_p3, stats, acc_a, acc_b = tied(from_p3, stats, acc_a, acc_b)
    stats = all_added(stats, next(rounds))
    (acc_a,) = stage(scalars, a, [from_p3], [None], acc_a)
    *from_r3, stats, acc_a, acc_b = tied(*from_r3, stats, acc_a, acc_b)
    stats = all_added(stats, next(rounds))
    outs = stage(
        scalars, b, [p3, *from_r3], [None, None, None], acc_b, final=(1, x, y, None)
    )

    last, outs, stats = tied(last, outs, stats)
    theirs = exchanged(stats, next(rounds))
    grad_image, grad_text = stage(
        scalars, a, [last], [None], acc_a, final=(0, x, y, tuple(outs))
    )
    sums = finished(scalars, stats, theirs, float(rows * count * STEPS))
    return grad_image, grad_text, sums


def solution(mesh):
    in_specs = (P("dp", None), P("dp", None), P(), P())
    out_specs = (P("dp", None), P("dp", None), P())
    return jax.shard_map(
        per_device, mesh=mesh, in_specs=in_specs, out_specs=out_specs, check_vma=False
    )
```

```python
import functools

import jax
import jax.numpy as jnp
from jax import lax
from jax.experimental import pallas as pl
from jax.experimental.pallas import tpu as pltpu
from jax.sharding import PartitionSpec as P

STEPS = 8
EPS = 1e-06
LOG2_E = 1.4426950408889634
LN_2 = 0.6931471805599453
ROUNDS = ((16,), (32,), (64,), (128,), (2,), (4,), (14,), 1)
VMEM_LIMIT = 24 * 1024 * 1024
SMEM = pl.BlockSpec(memory_space=pltpu.SMEM)
VMEM = pl.BlockSpec(memory_space=pltpu.VMEM)
HBM = pl.BlockSpec(memory_space=pltpu.HBM)


def my_core():
    return lax.rem(lax.axis_index("dp"), 2)


def inverse_norm(values):
    return lax.rsqrt(jnp.sum(values * values, axis=-1, keepdims=True) + EPS)


def fetch_own(x_ref, y_ref, raw, sems, want_image):
    pieces = sems.shape[0]
    size = raw.shape[0] // pieces
    for i in range(pieces):
        part = pl.ds(i * size, size)

        @pl.when(want_image)
        def _():
            pltpu.make_async_copy(x_ref.at[part], raw.at[part], sems.at[i]).start()

        @pl.when(jnp.logical_not(want_image))
        def _():
            pltpu.make_async_copy(y_ref.at[part], raw.at[part], sems.at[i]).start()


def normalize_kernel(x_ref, y_ref, a_ref, b_ref, raw, sems):
    core = my_core()
    sides = ((a_ref, core == 0), (b_ref, core == 1))
    for side, (_, want_image) in enumerate(sides):
        fetch_own(x_ref, y_ref, raw.at[side], sems.at[side], want_image)
    pieces = sems.shape[1]
    size = raw.shape[1] // pieces
    for side, (out_ref, _) in enumerate(sides):
        for i in range(pieces):
            part = pl.ds(i * size, size)
            pltpu.make_async_copy(x_ref.at[part], raw.at[side, part], sems.at[side, i]).wait()
            for start in range(i * size, (i + 1) * size, 48):
                block = slice(start, start + 48)
                values = raw[side, block, :].astype(jnp.float32)
                out_ref[block, :] = (values * inverse_norm(values)).astype(jnp.bfloat16)


def normalized(x, y):
    return pl.pallas_call(
        normalize_kernel,
        out_shape=[jax.ShapeDtypeStruct(x.shape, jnp.bfloat16)] * 2,
        in_specs=[HBM, HBM],
        out_specs=[VMEM, VMEM],
        scratch_shapes=[pltpu.VMEM((2, *x.shape), jnp.bfloat16), pltpu.SemaphoreType.DMA((2, 2))],
        compiler_params=pltpu.CompilerParams(vmem_limit_bytes=VMEM_LIMIT),
        cost_estimate=pl.CostEstimate(flops=1, bytes_accessed=1, transcendentals=0),
    )(x, y)


def folded(values):
    rows, columns = values.shape
    total = jnp.sum(values.reshape(rows // 8, 8, columns), axis=0)
    out = total[:, :128]
    for start in range(128, columns, 128):
        out = out + total[:, start : start + 128]
    return out


def negatives(sim, scalars, stats, weight):
    power = jnp.exp2(sim * scalars[2] + scalars[3])
    above = 1.0 + power
    inverse = pl.reciprocal(above, approx=True)
    inverse = inverse * (2.0 - above * inverse)
    grad = power * inverse
    if stats is not None:
        rest = (power - (above - 1.0)) * inverse
        parts = (folded(jnp.log2(above)), folded(rest), folded(grad * sim), folded(grad))
        for row, part in enumerate(parts):
            stats[row * 8 : row * 8 + 8, :] += part if weight is None else part * weight
    return scalars[0] * grad


def cut(blocks, width):
    pieces, current, room = [], [], width
    for index, rows in enumerate(blocks):
        start = 0
        while start < rows:
            take = min(room, rows - start)
            current.append((index, start, take))
            start, room = start + take, room - take
            if room == 0:
                pieces.append(current)
                current, room = [], width
    if current:
        pieces.append(current)
    return pieces


def joined(blocks, piece=None):
    if piece is None:
        piece = [(i, 0, block.shape[0]) for i, block in enumerate(blocks)]
    values = [blocks[i][start : start + take, :] for i, start, take in piece]
    return values[0] if len(values) == 1 else jnp.concatenate(values, axis=0)


def stage_kernel(plan, *refs):
    modes, label, has_acc, image_core, has_outs = plan
    refs = list(refs)
    scalars, own = refs.pop(0), refs.pop(0)
    blocks = [refs.pop(0) for _ in modes]
    acc_in = refs.pop(0) if has_acc else None
    if image_core is not None:
        x_ref, y_ref = refs.pop(0), refs.pop(0)
        if has_outs:
            refs = refs[2:]
        out_image, out_text = refs.pop(0), refs.pop(0)
    else:
        acc = refs.pop(0)
    stats = refs.pop(0) if any(m is not None for m in modes) else None
    tiles = refs.pop(0)
    core = my_core()
    if image_core is not None:
        acc, raw, sems, out_sems = refs
        is_image = core == image_core
        fetch_own(x_ref, y_ref, raw, sems, is_image)
    if stats is not None:
        stats[...] = jnp.zeros_like(stats)
    weight = core.astype(jnp.float32)
    weights = {"all": None, "core1": weight, "core0": 1.0 - weight}
    rows = own.shape[0]
    column = 0
    for piece in cut([block.shape[0] for block in blocks], 256):
        other = joined(blocks, piece)
        sim = lax.dot_general(
            own[...], other, (((1,), (1,)), ((), ())), preferred_element_type=jnp.float32
        )
        offset = 0
        for i, start, take in piece:
            part = sim[:, offset : offset + take]
            mode = modes[i]
            grad = negatives(part, scalars, None if mode is None else stats, weights.get(mode))
            if label and i == 0:
                across = lax.broadcasted_iota(jnp.int32, part.shape, 0)
                along = lax.broadcasted_iota(jnp.int32, part.shape, 1) + start
                positive = across == along
                if mode is not None:
                    zero = jnp.zeros_like(part)
                    logit = scalars[0] * part + scalars[1]
                    stats[8:16, :] -= folded(jnp.where(positive, logit, zero))
                    stats[16:24, :] -= folded(jnp.where(positive, part, zero))
                    stats[24:32, :] -= folded(positive.astype(jnp.float32))
                grad = jnp.where(positive, grad - scalars[0], grad)
            tiles[:, column : column + take] = grad.astype(jnp.bfloat16)
            offset, column = offset + take, column + take
    term = jnp.dot(tiles[...], joined(blocks), preferred_element_type=jnp.float32)
    acc[...] = term if acc_in is None else acc_in[...] + term
    if image_core is None:
        return
    pieces = sems.shape[0]
    size = rows // pieces
    for i in range(pieces):
        part = pl.ds(i * size, size)
        pltpu.make_async_copy(x_ref.at[part], raw.at[part], sems.at[i]).wait()
        for start in range(i * size, (i + 1) * size, 48):
            block = slice(start, start + 48)
            values = raw[block, :].astype(jnp.float32)
            inverse = inverse_norm(values)
            unit = values * inverse
            total = acc[block, :]
            acc[block, :] = inverse * (
                total - unit * jnp.sum(unit * total, axis=-1, keepdims=True)
            )

        @pl.when(is_image)
        def _():
            pltpu.make_async_copy(acc.at[part], out_image.at[part], out_sems.at[i]).start()

        @pl.when(jnp.logical_not(is_image))
        def _():
            pltpu.make_async_copy(acc.at[part], out_text.at[part], out_sems.at[i]).start()

    for i in range(pieces):
        part = pl.ds(i * size, size)
        pltpu.make_async_copy(acc.at[part], out_image.at[part], out_sems.at[i]).wait()


def middle_kernel(plan, *refs):
    scalars, stats = refs[0], refs[-1]
    blocks = refs[1:-1]
    odd = my_core() == 1
    stats[...] = jnp.zeros_like(stats)

    def chosen(pair):
        views = [blocks[i][start : start + size, :] for i, start, size in pair]
        return views[0] if len(views) == 1 else jnp.where(odd, views[0], views[1])

    for left, right in plan:
        one, other = chosen(left), chosen(right)
        for start in range(0, other.shape[0], 256):
            sim = lax.dot_general(
                one, other[start : start + 256], (((1,), (1,)), ((), ())),
                preferred_element_type=jnp.float32,
            )
            negatives(sim, scalars, stats, None)


def middle(scalars, blocks, plan):
    rows, width = blocks[0].shape
    pairs = sum(left[0][2] * right[0][2] for left, right in plan)
    return pl.pallas_call(
        functools.partial(middle_kernel, plan),
        out_shape=jax.ShapeDtypeStruct((32, 128), jnp.float32),
        in_specs=[SMEM] + [VMEM] * len(blocks),
        out_specs=VMEM,
        compiler_params=pltpu.CompilerParams(vmem_limit_bytes=VMEM_LIMIT),
        cost_estimate=pl.CostEstimate(flops=1, bytes_accessed=1, transcendentals=0),
    )(scalars, *blocks)


def stage(scalars, own, blocks, modes, acc=None, label=False, final=None):
    rows, width = own.shape
    big = jax.ShapeDtypeStruct((rows, width), jnp.float32)
    args, in_specs = [scalars, own, *blocks], [SMEM, VMEM] + [VMEM] * len(blocks)
    scratch = [pltpu.VMEM((rows, sum(block.shape[0] for block in blocks)), jnp.bfloat16)]
    aliases, image_core, has_outs = {}, None, False
    if acc is not None:
        args.append(acc)
        in_specs.append(VMEM)
    if final is None:
        if acc is not None:
            aliases = {len(args) - 1: 0}
        out_shape, out_specs = [big], [VMEM]
    else:
        image_core, x, y, outs = final
        args += [x, y]
        in_specs += [HBM, HBM]
        if outs is not None:
            has_outs = True
            aliases = {len(args): 0, len(args) + 1: 1}
            args += list(outs)
            in_specs += [HBM, HBM]
        out_shape, out_specs = [big, big], [HBM, HBM]
        scratch += [
            pltpu.VMEM((rows, width), jnp.float32),
            pltpu.VMEM((rows, width), jnp.bfloat16),
            pltpu.SemaphoreType.DMA((4,)),
            pltpu.SemaphoreType.DMA((4,)),
        ]
    if any(m is not None for m in modes):
        out_shape.append(jax.ShapeDtypeStruct((32, 128), jnp.float32))
        out_specs.append(VMEM)
    plan = (tuple(modes), label, acc is not None, image_core, has_outs)
    pairs = rows * sum(block.shape[0] for block in blocks)
    return pl.pallas_call(
        functools.partial(stage_kernel, plan),
        out_shape=out_shape,
        in_specs=in_specs,
        out_specs=out_specs,
        scratch_shapes=scratch,
        input_output_aliases=aliases,
        compiler_params=pltpu.CompilerParams(vmem_limit_bytes=VMEM_LIMIT),
        cost_estimate=pl.CostEstimate(flops=1, bytes_accessed=1, transcendentals=0),
    )(*args)


def finish_kernel(divisor, scalars, mine, theirs, out_ref):
    total = mine[...] + theirs[...]
    sums = [jnp.sum(total[row : row + 8, :]) for row in range(0, 32, 8)]
    out_ref[0] = (sums[0] * LN_2 + sums[1]) / divisor
    out_ref[1] = sums[2] * scalars[0] / divisor
    out_ref[2] = sums[3] / divisor


def finished(scalars, mine, theirs, divisor):
    return pl.pallas_call(
        functools.partial(finish_kernel, divisor),
        out_shape=jax.ShapeDtypeStruct((3,), jnp.float32),
        in_specs=[SMEM, VMEM, VMEM],
        out_specs=SMEM,
    )(scalars, mine, theirs)


def tied(*values):
    return lax.optimization_barrier(values)


def per_device(image_feats, text_feats, log_scale, bias):
    count = lax.axis_size("dp")
    up_down = [(d, (d + 2 if d % 2 else d - 2) % count) for d in range(count)]
    down_up = [(d, (d - 2 if d % 2 else d + 2) % count) for d in range(count)]
    cross = [(d, (d + 1 if d % 2 else d - 1) % count) for d in range(count)]
    other_core = [(d, d ^ 1) for d in range(count)]
    scale = jnp.exp(log_scale)
    scalars = jnp.stack([scale, bias, scale * LOG2_E, bias * LOG2_E])
    x = pltpu.with_memory_space_constraint(image_feats, pltpu.HBM)
    y = pltpu.with_memory_space_constraint(text_feats, pltpu.HBM)
    rows = image_feats.shape[0]
    half = rows // 2

    def up(value):
        return lax.ppermute(value, "dp", up_down)

    def down(value):
        return lax.ppermute(value, "dp", down_up)

    def swap(value):
        return lax.ppermute(value, "dp", other_core)

    def exchanged(value, distance):
        return lax.ppermute(value, "dp", [(d, d ^ distance) for d in range(count)])

    def all_added(value, distances):
        for distance in distances:
            if distance < count:
                value = value + exchanged(value, distance)
        return value

    whole = lambda i: (i, 0, rows)
    a, b = normalized(x, y)
    p1 = up(a)
    sibling = swap(b)
    acc_a, stats0 = stage(scalars, a, [b], ["all"], label=True)
    acc_b, stats1 = stage(scalars, b, [a, sibling], [None, "core1"], label=True)
    b, acc_a, acc_b = tied(b, acc_a, acc_b)
    r1 = down(b)

    p1, acc_a, acc_b = tied(p1, acc_a, acc_b)
    p2, from_p1 = up(p1), swap(p1)
    acc_b, stats2 = stage(scalars, b, [p1], ["all"], acc_b)

    r1, acc_b = tied(r1, acc_b)
    r2, from_r1 = down(r1), swap(r1)
    (acc_a,) = stage(scalars, a, [r1], [None], acc_a)
    stats3 = middle(scalars, [p1, r1], (((whole(0),), (whole(1),)),))

    p2, from_p1, acc_a, stats3 = tied(p2, from_p1, acc_a, stats3)
    p3, from_p2 = up(p2), swap(p2)
    acc_a, stats4 = stage(scalars, a, [from_p1], ["core0"], acc_a)
    stats5 = middle(scalars, [p2, r1], (((whole(0),), (whole(1),)),))

    r2, from_r1, acc_a, stats5 = tied(r2, from_r1, acc_a, stats5)
    r3, from_r2 = down(r2), swap(r2)
    acc_b, stats6 = stage(scalars, b, [from_r1], ["core1"], acc_b)
    stats7 = middle(
        scalars, [p1, r1, p2, r2, from_p1, from_r1, from_p2],
        (
            ((whole(0), whole(1)), (whole(4), whole(5))),
            ((whole(2), whole(3)), (whole(4), whole(5))),
            (((2, 0, half), (6, half, half)), (whole(6), whole(2))),
        ),
    )
    stats = (stats0 + stats1 + stats2 + stats3) + (stats4 + stats5 + stats6 + stats7)
    rounds = iter(ROUNDS)
    stats, acc_a, acc_b = tied(stats, acc_a, acc_b)
    stats = all_added(stats, next(rounds))
    (acc_a,) = stage(scalars, a, [r2], [None], acc_a)
    stats, acc_a, acc_b = tied(stats, acc_a, acc_b)
    stats = all_added(stats, next(rounds))
    (acc_a,) = stage(scalars, a, [from_p2], [None], acc_a)

    p3, acc_a, acc_b, stats = tied(p3, acc_a, acc_b, stats)
    last, from_p3 = lax.ppermute(p3, "dp", cross), swap(p3)
    stats = all_added(stats, next(rounds))
    (acc_b,) = stage(scalars, b, [p2], [None], acc_b)
    from_r2, stats, acc_a, acc_b = tied(from_r2, stats, acc_a, acc_b)
    stats = all_added(stats, next(rounds))
    (acc_b,) = stage(scalars, b, [from_r2], [None], acc_b)

    r3, acc_a, acc_b, stats = tied(r3, acc_a, acc_b, stats)
    from_r3 = [swap(r3[:half]), swap(r3[half:])]
    stats = all_added(stats, next(rounds))
    (acc_a,) = stage(scalars, a, [r3], [None], acc_a)
    from_p3, stats, acc_a, acc_b = tied(from_p3, stats, acc_a, acc_b)
    stats = all_added(stats, next(rounds))
    (acc_a,) = stage(scalars, a, [from_p3], [None], acc_a)
    *from_r3, stats, acc_a, acc_b = tied(*from_r3, stats, acc_a, acc_b)
    stats = all_added(stats, next(rounds))
    outs = stage(
        scalars, b, [p3, *from_r3], [None, None, None], acc_b, final=(1, x, y, None)
    )

    last, outs, stats = tied(last, outs, stats)
    theirs = exchanged(stats, next(rounds))
    grad_image, grad_text = stage(
        scalars, a, [last], [None], acc_a, final=(0, x, y, tuple(outs))
    )
    sums = finished(scalars, stats, theirs, float(rows * count * STEPS))
    return grad_image, grad_text, sums


def solution(mesh):
    in_specs = (P("dp", None), P("dp", None), P(), P())
    out_specs = (P("dp", None), P("dp", None), P())
    return jax.shard_map(
        per_device, mesh=mesh, in_specs=in_specs, out_specs=out_specs, check_vma=False
    )
```
